32 devices in a mesh: tm: 8 (over z, x), chan: 4 (over y, core).
Axes of the slice: x: 2, y: 2, z: 4, core: 2. Of those that a mesh axis runs over, the one named last changes fastest.
Arguments:
- features: bfloat16 [49152, 512], P('tm', 'chan'), may hold values from -6 to 6
- snake_alpha: float32 [512], P('chan'), may hold values from 0.5 to 3
- down_weight: bfloat16 [512, 16, 1024], P(None, None, 'chan'), may hold values from -0.0625 to 0.0625
- grad_out: bfloat16 [6144, 1024], P('tm', 'chan'), may hold values from -6 to 6
Outputs:
- encoded: bfloat16 [6144, 1024], P('tm', 'chan')
- grad_features: bfloat16 [49152, 512], P('tm', 'chan')
- grad_down: bfloat16 [1024, 16, 512], P('tm', None, 'chan')
The draws below stay inside these ranges and needn't reach their ends.
All inputs are finite; a program needn't handle non-finite values.
Results may differ from the reference program's by a relative error of at most 0.0049.
Values may be sent and summed in bfloat16 or wider, within the bound.
A program may use at most 128 MiB of HBM per device.

```python
import math
import jax
import jax.numpy as jnp

C = 512
OUTC = 1024
STRIDE = 8
FRAMES = 49152
OUT_FRAMES = 6144


def level_of(own_key, extent, pieces, least, high):
    level, own = 1.0, jax.random.fold_in(own_key, 6)
    for axis_at, parts in pieces:
        heights = jnp.exp(jax.random.uniform(jax.random.fold_in(own, axis_at), (parts,), jnp.float32, least / len(pieces), high / len(pieces)))
        level = level * jnp.repeat(heights, extent[axis_at] // parts).reshape([-1 if axis == axis_at else 1 for axis in range(len(extent))])
    return level


def centred(key, dims, scale, bound, split=(), kind=jnp.bfloat16):
    level = level_of(key, dims, split, -0.22, 0.18) if split else 1.0
    array = jax.random.normal(key, dims, jnp.float32) * scale * level
    return jnp.minimum(jnp.maximum(array, -bound), bound).astype(kind)


def setup_inputs(seed: int = 0) -> dict:
    streams_of = jax.random.split(jax.random.key(seed), 5)
    features = centred(streams_of[0], (FRAMES, C), 1.0, 6.0, ((0, 8), (1, 4)))
    snake_alpha = jnp.clip(jnp.exp(math.log(3.0) - 1.7917595 * jax.random.uniform(streams_of[1], (C,), jnp.float32) ** level_of(streams_of[1], (C,), ((0, 4),), -0.2, 0.2)), 0.5, 3.0)
    down_weight = centred(streams_of[2], (C, 2 * STRIDE, OUTC), (2 * STRIDE * C) ** -0.5, 0.0625, ((2, 4),))
    grad_out = centred(streams_of[3], (OUT_FRAMES, OUTC), 1.0, 6.0, ((0, 8), (1, 4)))
    return dict(features=features, snake_alpha=snake_alpha, down_weight=down_weight, grad_out=grad_out)


def snake(values, alpha):
    return values + jnp.sin(alpha * values) ** 2 / alpha

def reference(features, snake_alpha, down_weight, grad_out):
    wide = features.astype(jnp.float32)
    snaked = snake(wide, snake_alpha).astype(jnp.bfloat16)
    half = STRIDE // 2
    padded = jnp.pad(snaked, ((half, half), (0, 0)))
    tiled = padded.reshape(OUT_FRAMES + 1, STRIDE * C)
    early = jnp.transpose(down_weight[:, :STRIDE], (1, 0, 2)).reshape(STRIDE * C, OUTC)
    late = jnp.transpose(down_weight[:, STRIDE:], (1, 0, 2)).reshape(STRIDE * C, OUTC)
    encoded = (jnp.dot(tiled[:-1], early, preferred_element_type=jnp.float32) + jnp.dot(tiled[1:], late, preferred_element_type=jnp.float32)).astype(jnp.bfloat16)
    grad_pad = jnp.pad(grad_out, ((1, 1), (0, 0)))
    spread = jnp.dot(grad_pad[1:], early.T, preferred_element_type=jnp.float32) + jnp.dot(grad_pad[:-1], late.T, preferred_element_type=jnp.float32)
    grad_snaked = spread.reshape(FRAMES + STRIDE, C)[half:half + FRAMES]
    grad_features = (grad_snaked * (1.0 + jnp.sin(2.0 * snake_alpha * wide))).astype(jnp.bfloat16)
    lower = jnp.dot(tiled[:-1].T, grad_out, preferred_element_type=jnp.float32)
    upper = jnp.dot(tiled[1:].T, grad_out, preferred_element_type=jnp.float32)
    lower = jnp.transpose(lower.reshape(STRIDE, C, OUTC), (2, 0, 1))
    upper = jnp.transpose(upper.reshape(STRIDE, C, OUTC), (2, 0, 1))
    scale = 1.0 / math.sqrt(OUT_FRAMES)
    grad_down = (jnp.concatenate([lower, upper], axis=1) * scale).astype(jnp.bfloat16)
    return (encoded, grad_features, grad_down)
```

```python
import functools
import math

import jax
import jax.numpy as jnp
from jax import lax
from jax.experimental import pallas as pl
from jax.experimental.pallas import tpu as pltpu
from jax.sharding import PartitionSpec as P

STRIDE = 8
TAPS = 16
HALO = 16
PARTS = 4
BF = jnp.bfloat16
F32 = jnp.float32

PI_HIGH = 3.140625
PI_LOW = math.pi - PI_HIGH


def bit_reversed(value, bits):
    out = 0
    for _ in range(bits):
        out = out * 2 + value % 2
        value //= 2
    return out


def sin_cos(angle):
    turns = jnp.floor(angle * (1.0 / math.pi) + 0.5)
    r = (angle - turns * PI_HIGH) - turns * PI_LOW
    q = r * r
    s = -1.0 / math.factorial(11)
    for n, sign in ((9, 1.0), (7, -1.0), (5, 1.0), (3, -1.0), (1, 1.0)):
        s = s * q + sign / math.factorial(n)
    c = 1.0 / math.factorial(12)
    for n, sign in ((10, -1.0), (8, 1.0), (6, -1.0), (4, 1.0), (2, -1.0), (0, 1.0)):
        c = c * q + sign / math.factorial(n)
    return s * r, c


def dot(a, b, dims):
    return lax.dot_general(a, b, (dims, ((), ())), preferred_element_type=F32)


def kernel(
    count, feat, alpha, weight, grad, enc_out, gf_out, gd_out,
    snaked, factor, cols, gfull, gturn, gprev, gnext, gwide,
    wstage, wsend, wbuf, acc, sends, recvs, esum, esend, erecv, ysend, yrecv,
    flow, fhigh, glow, ghigh, gdwide,
    fsem, gsem, wsem, hsem, rsem, esem,
):
    bits = count.bit_length() - 1
    frames, ci = feat.shape
    units, pb = grad.shape
    width = TAPS * ci
    chunk = width // PARTS
    outs = 4 * pb
    rows = outs // count
    t = lax.axis_index("tm")
    ch = lax.axis_index("chan")
    nxt = lax.rem(t + 1, count)
    prv = lax.rem(t + count - 1, count)

    def flip(value, bit):
        return value + bit - 2 * bit * (lax.rem(value // bit, 2))

    sib = flip(ch, 1)
    par = flip(ch, 2)
    opp = flip(sib, 2)
    peers = (None, sib, par, opp)

    def remote(src, dst, sems, i, **where):
        return pltpu.make_async_remote_copy(
            src_ref=src, dst_ref=dst, send_sem=sems.at[0, i], recv_sem=sems.at[1, i],
            device_id=where, device_id_type=pl.DeviceIdType.MESH,
        )

    barrier = pltpu.get_barrier_semaphore()
    greet = [dict(chan=sib), dict(chan=par), dict(chan=opp), dict(tm=nxt), dict(tm=prv)]
    greet += [dict(tm=flip(t, 1 << s)) for s in range(bits)]
    for where in greet:
        pl.semaphore_signal(barrier, inc=1, device_id=where, device_id_type=pl.DeviceIdType.MESH)
    pl.semaphore_wait(barrier, len(greet))

    g_par = remote(grad, gfull.at[ch], gsem, 0, chan=par)
    g_sib = remote(grad, gfull.at[ch], gsem, 1, chan=sib)
    g_fwd = remote(gfull.at[par], gfull.at[par], gsem, 2, chan=sib)
    f_up = remote(feat.at[pl.ds(frames - HALO, HALO)], flow, fsem, 0, tm=nxt)
    f_down = remote(feat.at[pl.ds(0, HALO)], fhigh, fsem, 1, tm=prv)
    g_par.start()
    g_sib.start()
    f_up.start()
    f_down.start()

    def turn(owner, dst):
        for half in range(pb // 128):
            lanes = pl.ds(half * 128, 128)
            wstage[...] = weight[pl.ds(owner * ci, ci), :, lanes].astype(F32).reshape(ci * TAPS, 128)
            for k in range(TAPS):
                dst[pl.ds(k * ci, ci), lanes] = wstage[pl.ds(k, ci, stride=TAPS), :].astype(BF)

    w_copies = {}
    for r in (2, 3, 1):
        turn(peers[r], wsend.at[r - 1])
        w_copies[r] = remote(wsend.at[r - 1], wbuf.at[ch], wsem, r - 1, chan=peers[r])
        w_copies[r].start()
    turn(ch, wbuf.at[ch])
    gfull[ch] = grad[...]

    a = alpha[...]
    inv = 1.0 / a

    def activate(x):
        wide = x.astype(F32)
        s, c = sin_cos(a * wide)
        return wide + s * s * inv, 1.0 + 2.0 * (s * c)

    step = 256

    def snake_step(i, _):
        at = pl.multiple_of(i * step, step)
        val, fac = activate(feat[pl.ds(at, step), :])
        snaked[pl.ds(pl.multiple_of(HALO + at, HALO), step), :] = val
        factor[pl.ds(at, step), :] = fac
        return 0

    lax.fori_loop(0, frames // step, snake_step, 0)

    g_par.wait_recv()
    g_fwd.start()

    f_up.wait_recv()
    f_down.wait_recv()
    low_on = jnp.where(t > 0, 1.0, 0.0)
    high_on = jnp.where(t < count - 1, 1.0, 0.0)
    snaked[pl.ds(0, HALO), :] = activate(flow[...])[0] * low_on
    snaked[pl.ds(HALO + frames, HALO), :] = activate(fhigh[...])[0] * high_on
    for k in range(TAPS):
        cols[:, pl.ds(k * ci, ci)] = snaked[
            pl.ds(HALO - STRIDE // 2 + k, units, stride=STRIDE), :
        ].astype(BF)

    g_sib.wait_recv()
    g_fwd.wait_recv()
    h_up = remote(gfull.at[:, pl.ds(units - HALO, HALO), :], glow, hsem, 0, tm=nxt)
    h_down = remote(gfull.at[:, pl.ds(0, HALO), :], ghigh, hsem, 1, tm=prv)
    h_up.start()
    h_down.start()

    for blk in range(4):
        for part in range(pb // 128):
            turned = gfull[blk, :, pl.ds(part * 128, 128)].astype(F32).T.astype(BF)
            first = blk * pb + part * 128
            size = min(rows, 128)
            for j in range(128 // size):
                p = first + j * size
                d, rest = p // rows, p % rows
                gturn[pl.ds(bit_reversed(d, bits) * rows + rest, size), :] = turned[
                    j * size : (j + 1) * size, :
                ]

    bit_of = [lax.rem(t // (1 << s), 2) for s in range(bits)]
    half = outs // 2
    other = pl.multiple_of((1 - bit_of[0]) * half, half)
    mine = pl.multiple_of(bit_of[0] * half, half)

    def stage(s, c):
        return remote(
            sends[s].at[c], recvs[s].at[c], rsem, s * PARTS + c, tm=flip(t, 1 << s)
        )

    def first_half(c, _):
        lanes = pl.ds(pl.multiple_of(c * chunk, chunk), chunk)
        sends[0][c] = dot(gturn[pl.ds(other, half), :], cols[:, lanes], ((1,), (0,))).astype(BF)
        stage(0, c).start()
        return 0

    lax.fori_loop(0, PARTS, first_half, 0)

    def second_half(c, _):
        lanes = pl.ds(pl.multiple_of(c * chunk, chunk), chunk)
        acc[c] = dot(gturn[pl.ds(mine, half), :], cols[:, lanes], ((1,), (0,)))
        return 0

    lax.fori_loop(0, PARTS, second_half, 0)

    scale = 1.0 / math.sqrt(units * count)

    base = [0]
    for s in range(1, bits):
        base.append(base[-1] + bit_of[s] * (half >> s))

    def advance(s, c):
        size = half >> s
        copy = stage(s, c)
        copy.wait_recv()
        if s + 1 < bits:
            nsize = size // 2
            keep = pl.multiple_of(base[s + 1], nsize)
            give = pl.multiple_of(base[s] + (1 - bit_of[s + 1]) * nsize, nsize)
            here = pl.multiple_of(bit_of[s + 1] * nsize, nsize)
            there = pl.multiple_of((1 - bit_of[s + 1]) * nsize, nsize)
            sends[s + 1][c] = (
                acc[c, pl.ds(give, nsize), :] + recvs[s][c, pl.ds(there, nsize), :].astype(F32)
            ).astype(BF)
            stage(s + 1, c).start()
            acc[c, pl.ds(keep, nsize), :] = acc[c, pl.ds(keep, nsize), :] + recvs[s][
                c, pl.ds(here, nsize), :
            ].astype(F32)
        else:
            held = pl.multiple_of(base[s], size)
            total = (acc[c, pl.ds(held, size), :] + recvs[s][c].astype(F32)) * scale
            taps = chunk // ci
            for j in range(taps):
                gdwide[pl.ds(c * taps + j, size, stride=TAPS), :] = total[:, j * ci : (j + 1) * ci]

    events = sorted(
        ((c + s * 1.3, s, c) for s in range(bits) for c in range(PARTS))
    )
    events = [(s, c) for _, s, c in events]

    def run(limit):
        while events and events[0][1] + events[0][0] <= limit:
            advance(*events.pop(0))

    run(2)

    h_up.wait_recv()
    h_down.wait_recv()

    def shifted(blk, _):
        gwide[pl.ds(0, HALO), :] = glow[blk].astype(F32) * low_on
        gwide[pl.ds(HALO, units), :] = gfull[blk].astype(F32)
        gwide[pl.ds(HALO + units, HALO), :] = ghigh[blk].astype(F32) * high_on
        gprev[blk] = gwide[pl.ds(HALO - 1, units), :].astype(BF)
        gnext[blk] = gwide[pl.ds(HALO + 1, units), :].astype(BF)
        return 0

    lax.fori_loop(0, 4, shifted, 0)

    for r in (1, 2, 3):
        w_copies[r].wait_recv()

    def encode(d, _):
        esum[d] = dot(cols[...], wbuf[d], ((1,), (0,)))
        return 0

    lax.fori_loop(0, 4, encode, 0)
    esend[0] = esum[sib].astype(BF)
    esend[1] = esum[opp].astype(BF)
    e_sib = remote(esend, erecv, esem, 0, chan=sib)
    e_par = remote(ysend, yrecv, esem, 1, chan=par)
    e_sib.start()

    run(3)

    e_sib.wait_recv()
    ysend[...] = (esum[par] + erecv[1].astype(F32)).astype(BF)
    e_par.start()

    quarter = 4 * ci
    tile = units // 3

    def spread(i, _):
        at = pl.multiple_of(i * tile, tile)
        us = pl.ds(at, tile)
        for lo, own, side, shift in ((0, 1, 3, gprev), (4, 2, 0, gnext)):
            total = jnp.zeros((tile, quarter), F32)
            for blk in range(4):
                total += dot(
                    gfull[blk, us, :], wbuf[blk, pl.ds(own * quarter, quarter), :], ((1,), (1,))
                )
                total += dot(
                    shift[blk, us, :], wbuf[blk, pl.ds(side * quarter, quarter), :], ((1,), (1,))
                )
            for j in range(4):
                snaked[pl.ds(at * STRIDE + lo + j, tile, stride=STRIDE), :] = total[
                    :, j * ci : (j + 1) * ci
                ]
        return 0

    lax.fori_loop(0, 3, spread, 0)

    def finish(i, _):
        at = pl.multiple_of(i * step, step)
        here = pl.ds(at, step)
        gf_out[here, :] = (snaked[here, :] * factor[here, :]).astype(BF)
        return 0

    lax.fori_loop(0, frames // step, finish, 0)

    e_par.wait_recv()
    enc_out[...] = (esum[ch] + erecv[0].astype(F32) + yrecv[...].astype(F32)).astype(BF)

    run(100)
    gd_out[...] = gdwide[...].reshape(rows, TAPS, ci).astype(BF)

    for copy in [g_par, g_sib, g_fwd, f_up, f_down, h_up, h_down, e_sib, e_par, *w_copies.values()]:
        copy.wait_send()
    for s in range(bits):
        for c in range(PARTS):
            stage(s, c).wait_send()


def shards(count, features, snake_alpha, down_weight, grad_out):
    frames, ci = features.shape
    units, pb = grad_out.shape
    width = TAPS * ci
    chunk = width // PARTS
    outs = 4 * pb
    rows = outs // count
    bits = count.bit_length() - 1
    half = outs // 2
    vm = pltpu.VMEM
    stages = [vm((PARTS, half >> s, chunk), BF) for s in range(bits)]
    sem = pltpu.SemaphoreType.DMA

    def body(*refs):
        ins, scratch = refs[:7], refs[7:]
        first, rest = scratch[:12], scratch[12:]
        sends, rest = rest[:bits], rest[bits:]
        recvs, rest = rest[:bits], rest[bits:]
        kernel(count, *ins, *first, sends, recvs, *rest)

    return pl.pallas_call(
        body,
        out_shape=(
            jax.ShapeDtypeStruct((units, pb), BF),
            jax.ShapeDtypeStruct((frames, ci), BF),
            jax.ShapeDtypeStruct((rows, TAPS, ci), BF),
        ),
        in_specs=[pl.BlockSpec(memory_space=vm)] * 4,
        out_specs=[pl.BlockSpec(memory_space=vm)] * 3,
        scratch_shapes=[
            vm((frames + 2 * HALO, ci), F32),
            vm((frames, ci), F32),
            vm((units, width), BF),
            vm((4, units, pb), BF),
            vm((outs, units), BF),
            vm((4, units, pb), BF),
            vm((4, units, pb), BF),
            vm((units + 2 * HALO, pb), F32),
            vm((width, 128), F32),
            vm((3, width, pb), BF),
            vm((4, width, pb), BF),
            vm((PARTS, half, chunk), F32),
            *stages,
            *stages,
            vm((4, units, pb), F32),
            vm((2, units, pb), BF),
            vm((2, units, pb), BF),
            vm((units, pb), BF),
            vm((units, pb), BF),
            vm((HALO, ci), BF),
            vm((HALO, ci), BF),
            vm((4, HALO, pb), BF),
            vm((4, HALO, pb), BF),
            vm((rows * TAPS, ci), F32),
            sem((2, 2)),
            sem((2, 3)),
            sem((2, 3)),
            sem((2, 2)),
            sem((2, bits * PARTS)),
            sem((2, 2)),
        ],
        compiler_params=pltpu.CompilerParams(
            collective_id=0, has_side_effects=True, vmem_limit_bytes=60 * 1024 * 1024
        ),
        cost_estimate=pl.CostEstimate(
            flops=6 * units * width * outs, bytes_accessed=4 * width * outs, transcendentals=0
        ),
        name="fused",
    )(features, snake_alpha.reshape(1, ci), down_weight, grad_out)


def solution(mesh):
    placed = (P("tm", "chan"), P("chan"), P(None, None, "chan"), P("tm", "chan"))
    return jax.shard_map(
        functools.partial(shards, mesh.shape["tm"]),
        mesh=mesh,
        in_specs=placed,
        out_specs=(P("tm", "chan"), P("tm", "chan"), P("tm", None, "chan")),
        check_vma=False,
    )
```

```python
import functools
import math

import jax
import jax.numpy as jnp
from jax import lax
from jax.experimental import pallas as pl
from jax.experimental.pallas import tpu as pltpu
from jax.sharding import PartitionSpec as P

STRIDE = 8
TAPS = 16
HALO = 16
PARTS = 8
BF = jnp.bfloat16
F32 = jnp.float32

PI_HIGH = 3.140625
PI_LOW = math.pi - PI_HIGH


def bit_reversed(value, bits):
    out = 0
    for _ in range(bits):
        out = out * 2 + value % 2
        value //= 2
    return out


def sin_cos(angle):
    turns = jnp.floor(angle * (1.0 / math.pi) + 0.5)
    r = (angle - turns * PI_HIGH) - turns * PI_LOW
    q = r * r
    s = -1.0 / math.factorial(11)
    for n, sign in ((9, 1.0), (7, -1.0), (5, 1.0), (3, -1.0), (1, 1.0)):
        s = s * q + sign / math.factorial(n)
    c = 1.0 / math.factorial(12)
    for n, sign in ((10, -1.0), (8, 1.0), (6, -1.0), (4, 1.0), (2, -1.0), (0, 1.0)):
        c = c * q + sign / math.factorial(n)
    return s * r, c


def dot(a, b, dims):
    return lax.dot_general(a, b, (dims, ((), ())), preferred_element_type=F32)


def kernel(
    count, feat, alpha, weight, grad, enc_out, gf_out, gd_out,
    snaked, factor, cols, gfull, gturn, gprev, gnext, gwide,
    wstage, wsend, whalf, wbuf, acc, sends, recvs, esum, esend, erecv, ysend, yrecv,
    flow, fhigh, glow, ghigh, gdwide,
    fsem, gsem, wsem, hsem, rsem, esem,
):
    bits = count.bit_length() - 1
    frames, ci = feat.shape
    units, pb = grad.shape
    width = TAPS * ci
    chunk = width // PARTS
    outs = 4 * pb
    rows = outs // count
    t = lax.axis_index("tm")
    ch = lax.axis_index("chan")
    nxt = lax.rem(t + 1, count)
    prv = lax.rem(t + count - 1, count)

    def flip(value, bit):
        return value + bit - 2 * bit * (lax.rem(value // bit, 2))

    sib = flip(ch, 1)
    par = flip(ch, 2)
    opp = flip(sib, 2)

    def remote(src, dst, sems, i, **where):
        return pltpu.make_async_remote_copy(
            src_ref=src, dst_ref=dst, send_sem=sems.at[0, i], recv_sem=sems.at[1, i],
            device_id=where, device_id_type=pl.DeviceIdType.MESH,
        )

    barrier = pltpu.get_barrier_semaphore()
    greet = [dict(chan=sib), dict(chan=par), dict(chan=opp), dict(tm=nxt), dict(tm=prv)]
    greet += [dict(tm=flip(t, 1 << s)) for s in range(bits)]
    for where in greet:
        pl.semaphore_signal(barrier, inc=1, device_id=where, device_id_type=pl.DeviceIdType.MESH)
    pl.semaphore_wait(barrier, len(greet))

    g_par = remote(grad, gfull.at[ch], gsem, 0, chan=par)
    g_sib = remote(grad, gfull.at[ch], gsem, 1, chan=sib)
    g_fwd = remote(gfull.at[par], gfull.at[par], gsem, 2, chan=sib)
    f_up = remote(feat.at[pl.ds(frames - HALO, HALO)], flow, fsem, 0, tm=nxt)
    f_down = remote(feat.at[pl.ds(0, HALO)], fhigh, fsem, 1, tm=prv)
    g_par.start()
    g_sib.start()
    f_up.start()
    f_down.start()

    def turn(owner, dst):
        for half in range(pb // 128):
            lanes = pl.ds(half * 128, 128)
            wstage[...] = weight[pl.ds(owner * ci, ci), :, lanes].astype(F32).reshape(ci * TAPS, 128)
            for k in range(TAPS):
                dst[pl.ds(k * ci, ci), lanes] = wstage[pl.ds(k, ci, stride=TAPS), :].astype(BF)

    share = flip(t, 2)
    hw = width // 2
    htap = TAPS // 2
    lot = lax.rem(t // 2, 2)

    def turn_half(owner, their, dst):
        for part in range(pb // 128):
            lanes = pl.ds(part * 128, 128)
            wstage[...] = weight[pl.ds(owner * ci, ci), :, lanes].astype(F32).reshape(ci * TAPS, 128)
            for k in range(htap):
                dst[pl.ds(k * ci, ci), lanes] = wstage[
                    pl.ds(their * htap + k, ci, stride=TAPS), :
                ].astype(BF)

    got = pl.ds(pl.multiple_of(lot * hw, hw), hw)
    w_par = remote(whalf.at[0], wbuf.at[ch, got], wsem, 1, chan=par)
    w_opp = remote(whalf.at[1], wbuf.at[ch, got], wsem, 2, chan=opp)
    w_par_on = remote(wbuf.at[par, got], wbuf.at[par, got], wsem, 3, tm=share)
    w_opp_on = remote(wbuf.at[opp, got], wbuf.at[opp, got], wsem, 4, tm=share)
    w_sib = remote(wsend, wbuf.at[ch], wsem, 0, chan=sib)
    turn_half(par, lot, whalf.at[0])
    gfull[ch] = grad[...]

    a = alpha[...]
    inv = 1.0 / a

    def activate(x):
        wide = x.astype(F32)
        s, c = sin_cos(a * wide)
        return wide + s * s * inv, 1.0 + 2.0 * (s * c)

    step = 256

    def snake_step(i, _):
        at = pl.multiple_of(i * step, step)
        val, fac = activate(feat[pl.ds(at, step), :])
        snaked[pl.ds(pl.multiple_of(HALO + at, HALO), step), :] = val
        factor[pl.ds(at, step), :] = fac
        return 0

    lax.fori_loop(0, frames // step, snake_step, 0)

    f_up.wait_recv()
    f_down.wait_recv()
    low_on = jnp.where(t > 0, 1.0, 0.0)
    high_on = jnp.where(t < count - 1, 1.0, 0.0)
    snaked[pl.ds(0, HALO), :] = activate(flow[...])[0] * low_on
    snaked[pl.ds(HALO + frames, HALO), :] = activate(fhigh[...])[0] * high_on
    for k in range(TAPS):
        cols[:, pl.ds(k * ci, ci)] = snaked[
            pl.ds(HALO - STRIDE // 2 + k, units, stride=STRIDE), :
        ].astype(BF)

    def turn_grad(blk):
        for part in range(pb // 128):
            turned = gfull[blk, :, pl.ds(part * 128, 128)].astype(F32).T.astype(BF)
            size = min(rows, 128)
            for j in range(128 // size):
                p = blk * pb + part * 128 + j * size
                to = bit_reversed(p // rows, bits) * rows + p % rows
                gturn[pl.ds(pl.multiple_of(to, size), size), :] = turned[
                    j * size : (j + 1) * size, :
                ]

    turn_grad(ch)
    g_sib.wait_recv()
    turn_grad(sib)
    turn_half(opp, lot, whalf.at[1])
    g_par.wait_recv()
    g_fwd.start()
    w_par.start()
    w_opp.start()
    turn_grad(par)
    g_fwd.wait_recv()
    h_up = remote(gfull.at[:, pl.ds(units - HALO, HALO), :], glow, hsem, 0, tm=nxt)
    h_down = remote(gfull.at[:, pl.ds(0, HALO), :], ghigh, hsem, 1, tm=prv)
    h_up.start()
    h_down.start()
    turn_grad(opp)

    bit_of = [lax.rem(t // (1 << s), 2) for s in range(bits)]
    half = outs // 2
    other = pl.multiple_of((1 - bit_of[0]) * half, half)
    mine = pl.multiple_of(bit_of[0] * half, half)

    def stage(s, c):
        return remote(
            sends[s].at[c], recvs[s].at[c], rsem, s * PARTS + c, tm=flip(t, 1 << s)
        )

    def first_half(c, _):
        lanes = pl.ds(pl.multiple_of(c * chunk, chunk), chunk)
        sends[0][c] = dot(gturn[pl.ds(other, half), :], cols[:, lanes], ((1,), (0,))).astype(BF)
        stage(0, c).start()
        return 0

    lax.fori_loop(0, PARTS, first_half, 0)

    def second_half(c, _):
        lanes = pl.ds(pl.multiple_of(c * chunk, chunk), chunk)
        acc[c] = dot(gturn[pl.ds(mine, half), :], cols[:, lanes], ((1,), (0,)))
        return 0

    lax.fori_loop(0, PARTS, second_half, 0)
    turn(sib, wsend)
    w_sib.start()
    turn(ch, wbuf.at[ch])

    scale = 1.0 / math.sqrt(units * count)

    base = [0]
    for s in range(1, bits):
        base.append(base[-1] + bit_of[s] * (half >> s))

    def advance(s, c):
        size = half >> s
        copy = stage(s, c)
        copy.wait_recv()
        if s + 1 < bits:
            nsize = size // 2
            keep = pl.multiple_of(base[s + 1], nsize)
            give = pl.multiple_of(base[s] + (1 - bit_of[s + 1]) * nsize, nsize)
            here = pl.multiple_of(bit_of[s + 1] * nsize, nsize)
            there = pl.multiple_of((1 - bit_of[s + 1]) * nsize, nsize)
            sends[s + 1][c] = (
                acc[c, pl.ds(give, nsize), :] + recvs[s][c, pl.ds(there, nsize), :].astype(F32)
            ).astype(BF)
            stage(s + 1, c).start()
            acc[c, pl.ds(keep, nsize), :] = acc[c, pl.ds(keep, nsize), :] + recvs[s][
                c, pl.ds(here, nsize), :
            ].astype(F32)
        else:
            held = pl.multiple_of(base[s], size)
            total = (acc[c, pl.ds(held, size), :] + recvs[s][c].astype(F32)) * scale
            taps = chunk // ci
            for j in range(taps):
                gdwide[pl.ds(c * taps + j, size, stride=TAPS), :] = total[:, j * ci : (j + 1) * ci]

    events = sorted(
        ((c + s * 0.9, s, c) for s in range(bits) for c in range(PARTS))
    )
    events = [(s, c) for _, s, c in events]

    def run(limit):
        while events and events[0][1] + events[0][0] * 0.9 <= limit:
            advance(*events.pop(0))

    w_par.wait_recv()
    w_par_on.start()
    run(1)

    h_up.wait_recv()
    h_down.wait_recv()

    def shifted(blk, _):
        gwide[pl.ds(0, HALO), :] = glow[blk].astype(F32) * low_on
        gwide[pl.ds(HALO, units), :] = gfull[blk].astype(F32)
        gwide[pl.ds(HALO + units, HALO), :] = ghigh[blk].astype(F32) * high_on
        gprev[blk] = gwide[pl.ds(HALO - 1, units), :].astype(BF)
        gnext[blk] = gwide[pl.ds(HALO + 1, units), :].astype(BF)
        return 0

    lax.fori_loop(0, 4, shifted, 0)

    w_opp.wait_recv()
    w_opp_on.start()
    run(3.5)
    w_sib.wait_recv()
    w_par_on.wait_recv()
    w_opp_on.wait_recv()

    def encode(d, _):
        esum[d] = dot(cols[...], wbuf[d], ((1,), (0,)))
        return 0

    lax.fori_loop(0, 4, encode, 0)
    esend[0] = esum[sib].astype(BF)
    esend[1] = esum[opp].astype(BF)
    e_sib = remote(esend, erecv, esem, 0, chan=sib)
    e_par = remote(ysend, yrecv, esem, 1, chan=par)
    e_sib.start()

    run(4)

    e_sib.wait_recv()
    ysend[...] = (esum[par] + erecv[1].astype(F32)).astype(BF)
    e_par.start()

    quarter = 4 * ci
    tile = units // 3

    run(4.5)

    def spread(i):
        at = i * tile
        us = pl.ds(at, tile)
        for lo, own, side, shift in ((0, 1, 3, gprev), (4, 2, 0, gnext)):
            total = jnp.zeros((tile, quarter), F32)
            for blk in range(4):
                total += dot(
                    gfull[blk, us, :], wbuf[blk, pl.ds(own * quarter, quarter), :], ((1,), (1,))
                )
                total += dot(
                    shift[blk, us, :], wbuf[blk, pl.ds(side * quarter, quarter), :], ((1,), (1,))
                )
            for j in range(4):
                snaked[pl.ds(at * STRIDE + lo + j, tile, stride=STRIDE), :] = total[
                    :, j * ci : (j + 1) * ci
                ]

    spread(0)
    run(5)
    spread(1)
    run(5.5)
    spread(2)
    run(6)

    def finish(i, _):
        at = pl.multiple_of(i * step, step)
        here = pl.ds(at, step)
        gf_out[here, :] = (snaked[here, :] * factor[here, :]).astype(BF)
        return 0

    lax.fori_loop(0, frames // step, finish, 0)

    e_par.wait_recv()
    enc_out[...] = (esum[ch] + erecv[0].astype(F32) + yrecv[...].astype(F32)).astype(BF)

    run(100)
    gd_out[...] = gdwide[...].reshape(rows, TAPS, ci).astype(BF)

    started = [g_par, g_sib, g_fwd, f_up, f_down, h_up, h_down, e_sib, e_par]
    for copy in started + [w_sib, w_par, w_opp, w_par_on, w_opp_on]:
        copy.wait_send()
    for s in range(bits):
        for c in range(PARTS):
            stage(s, c).wait_send()


def shards(count, features, snake_alpha, down_weight, grad_out):
    frames, ci = features.shape
    units, pb = grad_out.shape
    width = TAPS * ci
    chunk = width // PARTS
    outs = 4 * pb
    rows = outs // count
    bits = count.bit_length() - 1
    half = outs // 2
    vm = pltpu.VMEM
    stages = [vm((PARTS, half >> s, chunk), BF) for s in range(bits)]
    sem = pltpu.SemaphoreType.DMA

    def body(*refs):
        ins, scratch = refs[:7], refs[7:]
        first, rest = scratch[:13], scratch[13:]
        sends, rest = rest[:bits], rest[bits:]
        recvs, rest = rest[:bits], rest[bits:]
        kernel(count, *ins, *first, sends, recvs, *rest)

    return pl.pallas_call(
        body,
        out_shape=(
            jax.ShapeDtypeStruct((units, pb), BF),
            jax.ShapeDtypeStruct((frames, ci), BF),
            jax.ShapeDtypeStruct((rows, TAPS, ci), BF),
        ),
        in_specs=[pl.BlockSpec(memory_space=vm)] * 4,
        out_specs=[pl.BlockSpec(memory_space=vm)] * 3,
        scratch_shapes=[
            vm((frames + 2 * HALO, ci), F32),
            vm((frames, ci), F32),
            vm((units, width), BF),
            vm((4, units, pb), BF),
            vm((outs, units), BF),
            vm((4, units, pb), BF),
            vm((4, units, pb), BF),
            vm((units + 2 * HALO, pb), F32),
            vm((width, 128), F32),
            vm((width, pb), BF),
            vm((2, width // 2, pb), BF),
            vm((4, width, pb), BF),
            vm((PARTS, half, chunk), F32),
            *stages,
            *stages,
            vm((4, units, pb), F32),
            vm((2, units, pb), BF),
            vm((2, units, pb), BF),
            vm((units, pb), BF),
            vm((units, pb), BF),
            vm((HALO, ci), BF),
            vm((HALO, ci), BF),
            vm((4, HALO, pb), BF),
            vm((4, HALO, pb), BF),
            vm((rows * TAPS, ci), F32),
            sem((2, 2)),
            sem((2, 3)),
            sem((2, 5)),
            sem((2, 2)),
            sem((2, bits * PARTS)),
            sem((2, 2)),
        ],
        compiler_params=pltpu.CompilerParams(
            collective_id=0, has_side_effects=True, vmem_limit_bytes=60 * 1024 * 1024
        ),
        cost_estimate=pl.CostEstimate(
            flops=6 * units * width * outs, bytes_accessed=4 * width * outs, transcendentals=0
        ),
        name="fused",
    )(features, snake_alpha.reshape(1, ci), down_weight, grad_out)


def solution(mesh):
    placed = (P("tm", "chan"), P("chan"), P(None, None, "chan"), P("tm", "chan"))
    return jax.shard_map(
        functools.partial(shards, mesh.shape["tm"]),
        mesh=mesh,
        in_specs=placed,
        out_specs=(P("tm", "chan"), P("tm", "chan"), P("tm", None, "chan")),
        check_vma=False,
    )
```

```python
import functools
import math

import jax
import jax.numpy as jnp
from jax import lax
from jax.experimental import pallas as pl
from jax.experimental.pallas import tpu as pltpu
from jax.sharding import PartitionSpec as P

STRIDE = 8
TAPS = 16
HALO = 16
PARTS = 8
AHEAD = 2
BF = jnp.bfloat16
F32 = jnp.float32

PI_HIGH = 3.140625
PI_LOW = math.pi - PI_HIGH


def bit_reversed(value, bits):
    out = 0
    for _ in range(bits):
        out = out * 2 + value % 2
        value //= 2
    return out


def sin_cos(angle):
    turns = jnp.floor(angle * (1.0 / math.pi) + 0.5)
    r = (angle - turns * PI_HIGH) - turns * PI_LOW
    q = r * r
    s = -1.0 / math.factorial(11)
    for n, sign in ((9, 1.0), (7, -1.0), (5, 1.0), (3, -1.0), (1, 1.0)):
        s = s * q + sign / math.factorial(n)
    c = 1.0 / math.factorial(12)
    for n, sign in ((10, -1.0), (8, 1.0), (6, -1.0), (4, 1.0), (2, -1.0), (0, 1.0)):
        c = c * q + sign / math.factorial(n)
    return s * r, c


def dot(a, b, dims):
    return lax.dot_general(a, b, (dims, ((), ())), preferred_element_type=F32)


def kernel(
    count, feat, alpha, weight, grad, enc_out, gf_out, gd_out,
    snaked, factor, cols, gfull, gturn, gprev, gnext, gwide,
    wstage, wsend, whalf, wbuf, acc, sends, recvs, esum, esend, erecv, ysend, yrecv,
    flow, fhigh, glow, ghigh, gdwide,
    fsem, gsem, wsem, hsem, rsem, esem,
):
    bits = count.bit_length() - 1
    frames, ci = feat.shape
    units, pb = grad.shape
    width = TAPS * ci
    chunk = width // PARTS
    outs = 4 * pb
    rows = outs // count
    t = lax.axis_index("tm")
    ch = lax.axis_index("chan")
    nxt = lax.rem(t + 1, count)
    prv = lax.rem(t + count - 1, count)

    def flip(value, bit):
        return value + bit - 2 * bit * (lax.rem(value // bit, 2))

    sib = flip(ch, 1)
    par = flip(ch, 2)
    opp = flip(sib, 2)

    def remote(src, dst, sems, i, **where):
        return pltpu.make_async_remote_copy(
            src_ref=src, dst_ref=dst, send_sem=sems.at[0, i], recv_sem=sems.at[1, i],
            device_id=where, device_id_type=pl.DeviceIdType.MESH,
        )

    barrier = pltpu.get_barrier_semaphore()
    greet = [dict(chan=sib), dict(chan=par), dict(chan=opp), dict(tm=nxt), dict(tm=prv)]
    greet += [dict(tm=flip(t, 1 << s)) for s in range(bits)]
    for where in greet:
        pl.semaphore_signal(barrier, inc=1, device_id=where, device_id_type=pl.DeviceIdType.MESH)
    pl.semaphore_wait(barrier, len(greet))

    g_par = remote(grad, gfull.at[ch], gsem, 0, chan=par)
    g_sib = remote(grad, gfull.at[ch], gsem, 1, chan=sib)
    g_fwd = remote(gfull.at[par], gfull.at[par], gsem, 2, chan=sib)
    f_up = remote(feat.at[pl.ds(frames - HALO, HALO)], flow, fsem, 0, tm=nxt)
    f_down = remote(feat.at[pl.ds(0, HALO)], fhigh, fsem, 1, tm=prv)
    g_par.start()
    g_sib.start()
    f_up.start()
    f_down.start()

    def turn(owner, dst):
        for half in range(pb // 128):
            lanes = pl.ds(half * 128, 128)
            wstage[...] = weight[pl.ds(owner * ci, ci), :, lanes].astype(F32).reshape(ci * TAPS, 128)
            for k in range(TAPS):
                dst[pl.ds(k * ci, ci), lanes] = wstage[pl.ds(k, ci, stride=TAPS), :].astype(BF)

    share = flip(t, 2)
    hw = width // 2
    htap = TAPS // 2
    lot = lax.rem(t // 2, 2)

    def turn_half(owner, their, dst):
        for part in range(pb // 128):
            lanes = pl.ds(part * 128, 128)
            wstage[...] = weight[pl.ds(owner * ci, ci), :, lanes].astype(F32).reshape(ci * TAPS, 128)
            for k in range(htap):
                dst[pl.ds(k * ci, ci), lanes] = wstage[
                    pl.ds(their * htap + k, ci, stride=TAPS), :
                ].astype(BF)

    got = pl.ds(pl.multiple_of(lot * hw, hw), hw)
    w_par = remote(whalf.at[0], wbuf.at[ch, got], wsem, 1, chan=par)
    w_opp = remote(whalf.at[1], wbuf.at[ch, got], wsem, 2, chan=opp)
    w_par_on = remote(wbuf.at[par, got], wbuf.at[par, got], wsem, 3, tm=share)
    w_opp_on = remote(wbuf.at[opp, got], wbuf.at[opp, got], wsem, 4, tm=share)
    w_sib = remote(wsend, wbuf.at[ch], wsem, 0, chan=sib)
    turn_half(par, lot, whalf.at[0])
    w_par.start()
    turn_half(opp, lot, whalf.at[1])
    w_opp.start()
    turn(sib, wsend)
    w_sib.start()
    gfull[ch] = grad[...]

    a = alpha[...]
    inv = 1.0 / a

    def activate(x):
        wide = x.astype(F32)
        s, c = sin_cos(a * wide)
        return wide + s * s * inv, 1.0 + 2.0 * (s * c)

    step = 256

    def snake_step(i, _):
        at = pl.multiple_of(i * step, step)
        val, fac = activate(feat[pl.ds(at, step), :])
        snaked[pl.ds(pl.multiple_of(HALO + at, HALO), step), :] = val
        factor[pl.ds(at, step), :] = fac
        return 0

    lax.fori_loop(0, frames // step, snake_step, 0)

    f_up.wait_recv()
    f_down.wait_recv()
    low_on = jnp.where(t > 0, 1.0, 0.0)
    high_on = jnp.where(t < count - 1, 1.0, 0.0)
    snaked[pl.ds(0, HALO), :] = activate(flow[...])[0] * low_on
    snaked[pl.ds(HALO + frames, HALO), :] = activate(fhigh[...])[0] * high_on
    for k in range(TAPS):
        cols[:, pl.ds(k * ci, ci)] = snaked[
            pl.ds(HALO - STRIDE // 2 + k, units, stride=STRIDE), :
        ].astype(BF)

    def turn_grad(blk):
        for part in range(pb // 128):
            turned = gfull[blk, :, pl.ds(part * 128, 128)].astype(F32).T.astype(BF)
            size = min(rows, 128)
            for j in range(128 // size):
                p = blk * pb + part * 128 + j * size
                to = bit_reversed(p // rows, bits) * rows + p % rows
                gturn[pl.ds(pl.multiple_of(to, size), size), :] = turned[
                    j * size : (j + 1) * size, :
                ]

    turn_grad(ch)
    g_sib.wait_recv()
    turn_grad(sib)
    g_par.wait_recv()
    g_fwd.start()
    turn_grad(par)
    g_fwd.wait_recv()
    h_up = remote(gfull.at[:, pl.ds(units - HALO, HALO), :], glow, hsem, 0, tm=nxt)
    h_down = remote(gfull.at[:, pl.ds(0, HALO), :], ghigh, hsem, 1, tm=prv)
    h_up.start()
    h_down.start()
    turn_grad(opp)

    bit_of = [lax.rem(t // (1 << s), 2) for s in range(bits)]
    half = outs // 2
    other = pl.multiple_of((1 - bit_of[0]) * half, half)
    mine = pl.multiple_of(bit_of[0] * half, half)

    def stage(s, c):
        return remote(
            sends[s].at[c], recvs[s].at[c], rsem, s * PARTS + c, tm=flip(t, 1 << s)
        )

    def first_half(c, _):
        lanes = pl.ds(pl.multiple_of(c * chunk, chunk), chunk)
        sends[0][c] = dot(gturn[pl.ds(other, half), :], cols[:, lanes], ((1,), (0,))).astype(BF)
        return 0

    for c in range(AHEAD):
        first_half(c, 0)
        stage(0, c).start()
    w_par.wait_recv()
    w_par_on.start()
    lax.fori_loop(AHEAD, PARTS, first_half, 0)

    def second_half(c, _):
        lanes = pl.ds(pl.multiple_of(c * chunk, chunk), chunk)
        acc[c] = dot(gturn[pl.ds(mine, half), :], cols[:, lanes], ((1,), (0,)))
        return 0

    lax.fori_loop(0, PARTS, second_half, 0)
    turn(ch, wbuf.at[ch])

    scale = 1.0 / math.sqrt(units * count)

    base = [0]
    for s in range(1, bits):
        base.append(base[-1] + bit_of[s] * (half >> s))

    def advance(s, c):
        size = half >> s
        copy = stage(s, c)
        copy.wait_recv()
        if s == 0 and c + AHEAD < PARTS:
            stage(0, c + AHEAD).start()
        if s + 1 < bits:
            nsize = size // 2
            keep = pl.multiple_of(base[s + 1], nsize)
            give = pl.multiple_of(base[s] + (1 - bit_of[s + 1]) * nsize, nsize)
            here = pl.multiple_of(bit_of[s + 1] * nsize, nsize)
            there = pl.multiple_of((1 - bit_of[s + 1]) * nsize, nsize)
            sends[s + 1][c] = (
                acc[c, pl.ds(give, nsize), :] + recvs[s][c, pl.ds(there, nsize), :].astype(F32)
            ).astype(BF)
            stage(s + 1, c).start()
            acc[c, pl.ds(keep, nsize), :] = acc[c, pl.ds(keep, nsize), :] + recvs[s][
                c, pl.ds(here, nsize), :
            ].astype(F32)
        else:
            held = pl.multiple_of(base[s], size)
            total = (acc[c, pl.ds(held, size), :] + recvs[s][c].astype(F32)) * scale
            taps = chunk // ci
            for j in range(taps):
                gdwide[pl.ds(c * taps + j, size, stride=TAPS), :] = total[:, j * ci : (j + 1) * ci]

    events = sorted(
        ((c + s * 0.9, s, c) for s in range(bits) for c in range(PARTS))
    )
    events = [(s, c) for _, s, c in events]

    def run(limit):
        while events and events[0][1] + events[0][0] * 0.9 <= limit:
            advance(*events.pop(0))

    run(0)

    h_up.wait_recv()
    h_down.wait_recv()

    def shifted(blk, _):
        gwide[pl.ds(0, HALO), :] = glow[blk].astype(F32) * low_on
        gwide[pl.ds(HALO, units), :] = gfull[blk].astype(F32)
        gwide[pl.ds(HALO + units, HALO), :] = ghigh[blk].astype(F32) * high_on
        gprev[blk] = gwide[pl.ds(HALO - 1, units), :].astype(BF)
        gnext[blk] = gwide[pl.ds(HALO + 1, units), :].astype(BF)
        return 0

    lax.fori_loop(0, 4, shifted, 0)

    w_opp.wait_recv()
    w_opp_on.start()
    run(3)
    w_sib.wait_recv()
    w_par_on.wait_recv()
    w_opp_on.wait_recv()

    def encode(d, _):
        esum[d] = dot(cols[...], wbuf[d], ((1,), (0,)))
        return 0

    lax.fori_loop(0, 4, encode, 0)
    esend[0] = esum[sib].astype(BF)
    esend[1] = esum[opp].astype(BF)
    e_sib = remote(esend, erecv, esem, 0, chan=sib)
    e_par = remote(ysend, yrecv, esem, 1, chan=par)
    e_sib.start()

    run(4)

    e_sib.wait_recv()
    ysend[...] = (esum[par] + erecv[1].astype(F32)).astype(BF)
    e_par.start()

    quarter = 4 * ci
    tile = units // 3

    run(4.5)

    def spread(i):
        at = i * tile
        us = pl.ds(at, tile)
        for lo, own, side, shift in ((0, 1, 3, gprev), (4, 2, 0, gnext)):
            total = jnp.zeros((tile, quarter), F32)
            for blk in range(4):
                total += dot(
                    gfull[blk, us, :], wbuf[blk, pl.ds(own * quarter, quarter), :], ((1,), (1,))
                )
                total += dot(
                    shift[blk, us, :], wbuf[blk, pl.ds(side * quarter, quarter), :], ((1,), (1,))
                )
            for j in range(4):
                snaked[pl.ds(at * STRIDE + lo + j, tile, stride=STRIDE), :] = total[
                    :, j * ci : (j + 1) * ci
                ]

    spread(0)
    run(5)
    spread(1)
    run(5.5)
    spread(2)
    run(6)

    def finish(i, _):
        at = pl.multiple_of(i * step, step)
        here = pl.ds(at, step)
        gf_out[here, :] = (snaked[here, :] * factor[here, :]).astype(BF)
        return 0

    lax.fori_loop(0, frames // step, finish, 0)

    e_par.wait_recv()
    enc_out[...] = (esum[ch] + erecv[0].astype(F32) + yrecv[...].astype(F32)).astype(BF)

    run(100)
    gd_out[...] = gdwide[...].reshape(rows, TAPS, ci).astype(BF)

    started = [g_par, g_sib, g_fwd, f_up, f_down, h_up, h_down, e_sib, e_par]
    for copy in started + [w_sib, w_par, w_opp, w_par_on, w_opp_on]:
        copy.wait_send()
    for s in range(bits):
        for c in range(PARTS):
            stage(s, c).wait_send()


def shards(count, features, snake_alpha, down_weight, grad_out):
    frames, ci = features.shape
    units, pb = grad_out.shape
    width = TAPS * ci
    chunk = width // PARTS
    outs = 4 * pb
    rows = outs // count
    bits = count.bit_length() - 1
    half = outs // 2
    vm = pltpu.VMEM
    stages = [vm((PARTS, half >> s, chunk), BF) for s in range(bits)]
    sem = pltpu.SemaphoreType.DMA

    def body(*refs):
        ins, scratch = refs[:7], refs[7:]
        first, rest = scratch[:13], scratch[13:]
        sends, rest = rest[:bits], rest[bits:]
        recvs, rest = rest[:bits], rest[bits:]
        kernel(count, *ins, *first, sends, recvs, *rest)

    return pl.pallas_call(
        body,
        out_shape=(
            jax.ShapeDtypeStruct((units, pb), BF),
            jax.ShapeDtypeStruct((frames, ci), BF),
            jax.ShapeDtypeStruct((rows, TAPS, ci), BF),
        ),
        in_specs=[pl.BlockSpec(memory_space=vm)] * 4,
        out_specs=[pl.BlockSpec(memory_space=vm)] * 3,
        scratch_shapes=[
            vm((frames + 2 * HALO, ci), F32),
            vm((frames, ci), F32),
            vm((units, width), BF),
            vm((4, units, pb), BF),
            vm((outs, units), BF),
            vm((4, units, pb), BF),
            vm((4, units, pb), BF),
            vm((units + 2 * HALO, pb), F32),
            vm((width, 128), F32),
            vm((width, pb), BF),
            vm((2, width // 2, pb), BF),
            vm((4, width, pb), BF),
            vm((PARTS, half, chunk), F32),
            *stages,
            *stages,
            vm((4, units, pb), F32),
            vm((2, units, pb), BF),
            vm((2, units, pb), BF),
            vm((units, pb), BF),
            vm((units, pb), BF),
            vm((HALO, ci), BF),
            vm((HALO, ci), BF),
            vm((4, HALO, pb), BF),
            vm((4, HALO, pb), BF),
            vm((rows * TAPS, ci), F32),
            sem((2, 2)),
            sem((2, 3)),
            sem((2, 5)),
            sem((2, 2)),
            sem((2, bits * PARTS)),
            sem((2, 2)),
        ],
        compiler_params=pltpu.CompilerParams(
            collective_id=0, has_side_effects=True, vmem_limit_bytes=60 * 1024 * 1024
        ),
        cost_estimate=pl.CostEstimate(
            flops=6 * units * width * outs, bytes_accessed=4 * width * outs, transcendentals=0
        ),
        name="fused",
    )(features, snake_alpha.reshape(1, ci), down_weight, grad_out)


def solution(mesh):
    placed = (P("tm", "chan"), P("chan"), P(None, None, "chan"), P("tm", "chan"))
    return jax.shard_map(
        functools.partial(shards, mesh.shape["tm"]),
        mesh=mesh,
        in_specs=placed,
        out_specs=(P("tm", "chan"), P("tm", "chan"), P("tm", None, "chan")),
        check_vma=False,
    )
```

```python
import functools
import math

import jax
import jax.numpy as jnp
from jax import lax
from jax.experimental import pallas as pl
from jax.experimental.pallas import tpu as pltpu
from jax.sharding import PartitionSpec as P

STRIDE = 8
TAPS = 16
HALO = 16
PARTS = 8
BF = jnp.bfloat16
F32 = jnp.float32

PI_HIGH = 3.140625
PI_LOW = math.pi - PI_HIGH


def bit_reversed(value, bits):
    out = 0
    for _ in range(bits):
        out = out * 2 + value % 2
        value //= 2
    return out


def sin_cos(angle):
    turns = jnp.floor(angle * (1.0 / math.pi) + 0.5)
    r = (angle - turns * PI_HIGH) - turns * PI_LOW
    q = r * r
    s = -1.0 / math.factorial(11)
    for n, sign in ((9, 1.0), (7, -1.0), (5, 1.0), (3, -1.0), (1, 1.0)):
        s = s * q + sign / math.factorial(n)
    c = 1.0 / math.factorial(12)
    for n, sign in ((10, -1.0), (8, 1.0), (6, -1.0), (4, 1.0), (2, -1.0), (0, 1.0)):
        c = c * q + sign / math.factorial(n)
    return s * r, c


def dot(a, b, dims):
    return lax.dot_general(a, b, (dims, ((), ())), preferred_element_type=F32)


def kernel(
    count, feat, alpha, weight, grad, enc_out, gf_out, gd_out,
    snaked, factor, cols, gfull, gturn, gprev, gnext, gwide,
    wstage, wsend, wbuf, acc, sends, recvs, esum, esend, erecv, ysend, yrecv,
    flow, fhigh, glow, ghigh, gdwide,
    fsem, gsem, wsem, hsem, rsem, esem,
):
    bits = count.bit_length() - 1
    frames, ci = feat.shape
    units, pb = grad.shape
    width = TAPS * ci
    chunk = width // PARTS
    outs = 4 * pb
    rows = outs // count
    t = lax.axis_index("tm")
    ch = lax.axis_index("chan")
    nxt = lax.rem(t + 1, count)
    prv = lax.rem(t + count - 1, count)

    def flip(value, bit):
        return value + bit - 2 * bit * (lax.rem(value // bit, 2))

    sib = flip(ch, 1)
    par = flip(ch, 2)
    opp = flip(sib, 2)
    peers = (None, sib, par, opp)

    def remote(src, dst, sems, i, **where):
        return pltpu.make_async_remote_copy(
            src_ref=src, dst_ref=dst, send_sem=sems.at[0, i], recv_sem=sems.at[1, i],
            device_id=where, device_id_type=pl.DeviceIdType.MESH,
        )

    barrier = pltpu.get_barrier_semaphore()
    greet = [dict(chan=sib), dict(chan=par), dict(chan=opp), dict(tm=nxt), dict(tm=prv)]
    greet += [dict(tm=flip(t, 1 << s)) for s in range(bits)]
    for where in greet:
        pl.semaphore_signal(barrier, inc=1, device_id=where, device_id_type=pl.DeviceIdType.MESH)
    pl.semaphore_wait(barrier, len(greet))

    g_par = remote(grad, gfull.at[ch], gsem, 0, chan=par)
    g_sib = remote(grad, gfull.at[ch], gsem, 1, chan=sib)
    g_fwd = remote(gfull.at[par], gfull.at[par], gsem, 2, chan=sib)
    f_up = remote(feat.at[pl.ds(frames - HALO, HALO)], flow, fsem, 0, tm=nxt)
    f_down = remote(feat.at[pl.ds(0, HALO)], fhigh, fsem, 1, tm=prv)
    g_par.start()
    g_sib.start()
    f_up.start()
    f_down.start()

    def turn(owner, dst):
        for half in range(pb // 128):
            lanes = pl.ds(half * 128, 128)
            wstage[...] = weight[pl.ds(owner * ci, ci), :, lanes].astype(F32).reshape(ci * TAPS, 128)
            for k in range(TAPS):
                dst[pl.ds(k * ci, ci), lanes] = wstage[pl.ds(k, ci, stride=TAPS), :].astype(BF)

    w_copies = {}
    for r in (2, 3, 1):
        turn(peers[r], wsend.at[r - 1])
        w_copies[r] = remote(wsend.at[r - 1], wbuf.at[ch], wsem, r - 1, chan=peers[r])
        w_copies[r].start()
    gfull[ch] = grad[...]

    a = alpha[...]
    inv = 1.0 / a

    def activate(x):
        wide = x.astype(F32)
        s, c = sin_cos(a * wide)
        return wide + s * s * inv, 1.0 + 2.0 * (s * c)

    step = 256

    def snake_step(i, _):
        at = pl.multiple_of(i * step, step)
        val, fac = activate(feat[pl.ds(at, step), :])
        snaked[pl.ds(pl.multiple_of(HALO + at, HALO), step), :] = val
        factor[pl.ds(at, step), :] = fac
        return 0

    lax.fori_loop(0, frames // step, snake_step, 0)

    g_par.wait_recv()
    g_fwd.start()

    f_up.wait_recv()
    f_down.wait_recv()
    low_on = jnp.where(t > 0, 1.0, 0.0)
    high_on = jnp.where(t < count - 1, 1.0, 0.0)
    snaked[pl.ds(0, HALO), :] = activate(flow[...])[0] * low_on
    snaked[pl.ds(HALO + frames, HALO), :] = activate(fhigh[...])[0] * high_on
    for k in range(TAPS):
        cols[:, pl.ds(k * ci, ci)] = snaked[
            pl.ds(HALO - STRIDE // 2 + k, units, stride=STRIDE), :
        ].astype(BF)

    g_sib.wait_recv()
    g_fwd.wait_recv()
    h_up = remote(gfull.at[:, pl.ds(units - HALO, HALO), :], glow, hsem, 0, tm=nxt)
    h_down = remote(gfull.at[:, pl.ds(0, HALO), :], ghigh, hsem, 1, tm=prv)
    h_up.start()
    h_down.start()

    for blk in range(4):
        for part in range(pb // 128):
            turned = gfull[blk, :, pl.ds(part * 128, 128)].astype(F32).T.astype(BF)
            first = blk * pb + part * 128
            size = min(rows, 128)
            for j in range(128 // size):
                p = first + j * size
                d, rest = p // rows, p % rows
                gturn[pl.ds(bit_reversed(d, bits) * rows + rest, size), :] = turned[
                    j * size : (j + 1) * size, :
                ]

    bit_of = [lax.rem(t // (1 << s), 2) for s in range(bits)]
    half = outs // 2
    other = pl.multiple_of((1 - bit_of[0]) * half, half)
    mine = pl.multiple_of(bit_of[0] * half, half)

    def stage(s, c):
        return remote(
            sends[s].at[c], recvs[s].at[c], rsem, s * PARTS + c, tm=flip(t, 1 << s)
        )

    def first_half(c, _):
        lanes = pl.ds(pl.multiple_of(c * chunk, chunk), chunk)
        sends[0][c] = dot(gturn[pl.ds(other, half), :], cols[:, lanes], ((1,), (0,))).astype(BF)
        stage(0, c).start()
        return 0

    lax.fori_loop(0, PARTS, first_half, 0)

    def second_half(c, _):
        lanes = pl.ds(pl.multiple_of(c * chunk, chunk), chunk)
        acc[c] = dot(gturn[pl.ds(mine, half), :], cols[:, lanes], ((1,), (0,)))
        return 0

    lax.fori_loop(0, PARTS, second_half, 0)
    turn(ch, wbuf.at[ch])

    scale = 1.0 / math.sqrt(units * count)

    base = [0]
    for s in range(1, bits):
        base.append(base[-1] + bit_of[s] * (half >> s))

    def advance(s, c):
        size = half >> s
        copy = stage(s, c)
        copy.wait_recv()
        if s + 1 < bits:
            nsize = size // 2
            keep = pl.multiple_of(base[s + 1], nsize)
            give = pl.multiple_of(base[s] + (1 - bit_of[s + 1]) * nsize, nsize)
            here = pl.multiple_of(bit_of[s + 1] * nsize, nsize)
            there = pl.multiple_of((1 - bit_of[s + 1]) * nsize, nsize)
            sends[s + 1][c] = (
                acc[c, pl.ds(give, nsize), :] + recvs[s][c, pl.ds(there, nsize), :].astype(F32)
            ).astype(BF)
            stage(s + 1, c).start()
            acc[c, pl.ds(keep, nsize), :] = acc[c, pl.ds(keep, nsize), :] + recvs[s][
                c, pl.ds(here, nsize), :
            ].astype(F32)
        else:
            held = pl.multiple_of(base[s], size)
            total = (acc[c, pl.ds(held, size), :] + recvs[s][c].astype(F32)) * scale
            taps = chunk // ci
            for j in range(taps):
                gdwide[pl.ds(c * taps + j, size, stride=TAPS), :] = total[:, j * ci : (j + 1) * ci]

    events = sorted(
        ((c + s * 0.9, s, c) for s in range(bits) for c in range(PARTS))
    )
    events = [(s, c) for _, s, c in events]

    def run(limit):
        while events and events[0][1] + events[0][0] * 0.9 <= limit:
            advance(*events.pop(0))

    run(2)

    h_up.wait_recv()
    h_down.wait_recv()

    def shifted(blk, _):
        gwide[pl.ds(0, HALO), :] = glow[blk].astype(F32) * low_on
        gwide[pl.ds(HALO, units), :] = gfull[blk].astype(F32)
        gwide[pl.ds(HALO + units, HALO), :] = ghigh[blk].astype(F32) * high_on
        gprev[blk] = gwide[pl.ds(HALO - 1, units), :].astype(BF)
        gnext[blk] = gwide[pl.ds(HALO + 1, units), :].astype(BF)
        return 0

    lax.fori_loop(0, 4, shifted, 0)

    run(5)
    for r in (1, 2, 3):
        w_copies[r].wait_recv()

    def encode(d, _):
        esum[d] = dot(cols[...], wbuf[d], ((1,), (0,)))
        return 0

    lax.fori_loop(0, 4, encode, 0)
    esend[0] = esum[sib].astype(BF)
    esend[1] = esum[opp].astype(BF)
    e_sib = remote(esend, erecv, esem, 0, chan=sib)
    e_par = remote(ysend, yrecv, esem, 1, chan=par)
    e_sib.start()

    run(5.9)

    e_sib.wait_recv()
    ysend[...] = (esum[par] + erecv[1].astype(F32)).astype(BF)
    e_par.start()

    quarter = 4 * ci
    tile = units // 3

    def spread(i):
        at = i * tile
        us = pl.ds(at, tile)
        for lo, own, side, shift in ((0, 1, 3, gprev), (4, 2, 0, gnext)):
            total = jnp.zeros((tile, quarter), F32)
            for blk in range(4):
                total += dot(
                    gfull[blk, us, :], wbuf[blk, pl.ds(own * quarter, quarter), :], ((1,), (1,))
                )
                total += dot(
                    shift[blk, us, :], wbuf[blk, pl.ds(side * quarter, quarter), :], ((1,), (1,))
                )
            for j in range(4):
                snaked[pl.ds(at * STRIDE + lo + j, tile, stride=STRIDE), :] = total[
                    :, j * ci : (j + 1) * ci
                ]

    spread(0)
    run(6.9)
    spread(1)
    run(7.9)
    spread(2)
    run(8)

    def finish(i, _):
        at = pl.multiple_of(i * step, step)
        here = pl.ds(at, step)
        gf_out[here, :] = (snaked[here, :] * factor[here, :]).astype(BF)
        return 0

    lax.fori_loop(0, frames // step, finish, 0)

    e_par.wait_recv()
    enc_out[...] = (esum[ch] + erecv[0].astype(F32) + yrecv[...].astype(F32)).astype(BF)

    run(100)
    gd_out[...] = gdwide[...].reshape(rows, TAPS, ci).astype(BF)

    for copy in [g_par, g_sib, g_fwd, f_up, f_down, h_up, h_down, e_sib, e_par, *w_copies.values()]:
        copy.wait_send()
    for s in range(bits):
        for c in range(PARTS):
            stage(s, c).wait_send()


def shards(count, features, snake_alpha, down_weight, grad_out):
    frames, ci = features.shape
    units, pb = grad_out.shape
    width = TAPS * ci
    chunk = width // PARTS
    outs = 4 * pb
    rows = outs // count
    bits = count.bit_length() - 1
    half = outs // 2
    vm = pltpu.VMEM
    stages = [vm((PARTS, half >> s, chunk), BF) for s in range(bits)]
    sem = pltpu.SemaphoreType.DMA

    def body(*refs):
        ins, scratch = refs[:7], refs[7:]
        first, rest = scratch[:12], scratch[12:]
        sends, rest = rest[:bits], rest[bits:]
        recvs, rest = rest[:bits], rest[bits:]
        kernel(count, *ins, *first, sends, recvs, *rest)

    return pl.pallas_call(
        body,
        out_shape=(
            jax.ShapeDtypeStruct((units, pb), BF),
            jax.ShapeDtypeStruct((frames, ci), BF),
            jax.ShapeDtypeStruct((rows, TAPS, ci), BF),
        ),
        in_specs=[pl.BlockSpec(memory_space=vm)] * 4,
        out_specs=[pl.BlockSpec(memory_space=vm)] * 3,
        scratch_shapes=[
            vm((frames + 2 * HALO, ci), F32),
            vm((frames, ci), F32),
            vm((units, width), BF),
            vm((4, units, pb), BF),
            vm((outs, units), BF),
            vm((4, units, pb), BF),
            vm((4, units, pb), BF),
            vm((units + 2 * HALO, pb), F32),
            vm((width, 128), F32),
            vm((3, width, pb), BF),
            vm((4, width, pb), BF),
            vm((PARTS, half, chunk), F32),
            *stages,
            *stages,
            vm((4, units, pb), F32),
            vm((2, units, pb), BF),
            vm((2, units, pb), BF),
            vm((units, pb), BF),
            vm((units, pb), BF),
            vm((HALO, ci), BF),
            vm((HALO, ci), BF),
            vm((4, HALO, pb), BF),
            vm((4, HALO, pb), BF),
            vm((rows * TAPS, ci), F32),
            sem((2, 2)),
            sem((2, 3)),
            sem((2, 3)),
            sem((2, 2)),
            sem((2, bits * PARTS)),
            sem((2, 2)),
        ],
        compiler_params=pltpu.CompilerParams(
            collective_id=0, has_side_effects=True, vmem_limit_bytes=60 * 1024 * 1024
        ),
        cost_estimate=pl.CostEstimate(
            flops=6 * units * width * outs, bytes_accessed=4 * width * outs, transcendentals=0
        ),
        name="fused",
    )(features, snake_alpha.reshape(1, ci), down_weight, grad_out)


def solution(mesh):
    placed = (P("tm", "chan"), P("chan"), P(None, None, "chan"), P("tm", "chan"))
    return jax.shard_map(
        functools.partial(shards, mesh.shape["tm"]),
        mesh=mesh,
        in_specs=placed,
        out_specs=(P("tm", "chan"), P("tm", "chan"), P("tm", None, "chan")),
        check_vma=False,
    )
```
